32 devices in a mesh: seq: 16 (over z, y, x), mp: 2 (over core).
Axes of the slice: x: 2, y: 2, z: 4, core: 2. Of those that a mesh axis runs over, the one named last changes fastest.
Arguments:
- queries: bfloat16 [4096, 2048], P('seq', 'mp'), may hold values from -6 to 6
- keys: bfloat16 [4096, 2048], P('seq', 'mp'), may hold values from -6 to 6
- values: bfloat16 [4096, 2048], P('seq', 'mp'), may hold values from -20 to 20
- norm_gain: float32 [2048], P('mp'), may hold values from 0.1 to 1.9
- w_out: bfloat16 [2048, 4096], P('seq', 'mp'), may hold values from -0.125 to 0.125
Outputs:
- projected: bfloat16 [4096, 4096], P('seq', 'mp')
The draws below stay inside these ranges and needn't reach their ends.
All inputs are finite; a program needn't handle non-finite values.
Results may differ from the reference program's by a relative error of at most 0.0057.
Values may be sent and summed in bfloat16 or wider, within the bound.
No kernel may reach another device: no remote copies, remote signals or barrier semaphores. Data moves between devices by JAX's collectives and lax.ppermute only.
A program may use at most 192 MiB of HBM per device.

```python
import jax
import jax.numpy as jnp
from jax import lax

D = 4096
HEADS = 16
HD = 128
TOK_DEV = 256
INNER = 2048
TOKENS = 4096


def draw_values(key, part):
    base_key, scale_key = jax.random.split(jax.random.fold_in(key, 7))
    column_scale = jnp.exp(jax.random.uniform(scale_key, (1, INNER), jnp.float32, -1.2, 1.2))
    base = jnp.clip(jax.random.normal(base_key, (TOKENS, INNER), jnp.float32), -6.0, 6.0)
    return (base * column_scale).astype(jnp.bfloat16)


def block_levels(key, extent, shards, low, top_value):
    loudness, own = 1.0, jax.random.fold_in(key, 6)
    for axis_at, parts in shards:
        draws = jnp.exp(jax.random.uniform(jax.random.fold_in(own, axis_at), (parts,), jnp.float32, low / len(shards), top_value / len(shards)))
        loudness = loudness * jnp.repeat(draws, extent[axis_at] // parts).reshape([-1 if axis == axis_at else 1 for axis in range(len(extent))])
    return loudness


def bell_draw(own_key, dims, spread, limit, pieces=(), held_as=jnp.bfloat16):
    values = spread * jax.random.normal(own_key, dims, jnp.float32)
    if pieces:
        values = values * block_levels(own_key, dims, pieces, -0.22, 0.18)
    return jnp.clip(values, -limit, limit).astype(held_as)


def setup_inputs(seed: int = 0) -> dict:
    key_of = jax.random.split(jax.random.key(seed), 6)
    return {
        "queries": bell_draw(key_of[0], (TOKENS, INNER), 1.0, 6.0, ((0, 16), (1, 2))),
        "keys": bell_draw(key_of[1], (TOKENS, INNER), 1.0, 6.0, ((0, 16), (1, 2))),
        "values": draw_values(jax.random.fold_in(key_of[5], 71), 0),
        "norm_gain": jnp.clip(1.0 + 0.18 * jax.random.normal(key_of[3], (INNER,), jnp.float32), 0.1, 1.9),
        "w_out": bell_draw(key_of[4], (INNER, D), INNER ** -0.5, 0.125, ((0, 16), (1, 2))),
    }


def reference(queries, keys, values, norm_gain, w_out):
    blocks = queries.shape[0] // TOK_DEV
    q_all = queries.reshape(blocks, TOK_DEV, HEADS, HD)
    k_all = keys.reshape(blocks, TOK_DEV, HEADS, HD)
    v_all = values.reshape(blocks, TOK_DEV, HEADS, HD)
    gain = norm_gain.reshape(HEADS, HD)
    causal = jnp.arange(TOK_DEV)[:, None] >= jnp.arange(TOK_DEV)[None, :]

    def step(state, inputs):
        q_blk, k_blk, v_blk = inputs
        fq = jax.nn.silu(q_blk.astype(jnp.float32)).astype(jnp.bfloat16)
        fk = jax.nn.silu(k_blk.astype(jnp.float32)).astype(jnp.bfloat16)
        fq32 = fq.astype(jnp.float32)
        fk32 = fk.astype(jnp.float32)
        v32 = v_blk.astype(jnp.float32)
        scores = jnp.einsum('thd,shd->hts', fq32, fk32, precision=lax.Precision.HIGHEST)
        scores = jnp.where(causal[None], scores, 0.0).astype(jnp.bfloat16)
        intra = jnp.einsum('hts,shd->thd', scores.astype(jnp.float32), v32, precision=lax.Precision.HIGHEST)
        inter = jnp.einsum('thd,hde->the', fq32, state, precision=lax.Precision.HIGHEST)
        mixed = intra + inter
        scale = lax.rsqrt(lax.optimization_barrier(jnp.mean(mixed * mixed, axis=-1, keepdims=True)) + 1e-06)
        normed = (mixed * scale * gain[None]).astype(jnp.bfloat16).reshape(TOK_DEV, HEADS * HD)
        projected = jnp.dot(normed, w_out, preferred_element_type=jnp.float32).astype(jnp.bfloat16)
        own = jnp.einsum('thd,the->hde', fk32, v32, precision=lax.Precision.HIGHEST)
        return (state + own, projected)
    start = jnp.zeros((HEADS, HD, HD), jnp.float32)
    final, outputs = lax.scan(step, start, (q_all, k_all, v_all))
    return outputs.reshape(blocks * TOK_DEV, w_out.shape[1])
```

```python
import functools

import jax
import jax.numpy as jnp
from jax import lax
from jax.experimental import pallas as pl
from jax.experimental.pallas import tpu as pltpu
from jax.sharding import PartitionSpec as P

HD = 128
PLANE = 4
F32, BF16 = jnp.float32, jnp.bfloat16
VMEM_LIMIT = 40 * 1024 * 1024

ANY = pl.BlockSpec(memory_space=pl.ANY)
VMEM = pl.BlockSpec(memory_space=pltpu.VMEM)
SMEM = pl.BlockSpec(memory_space=pltpu.SMEM)


def call(body, outs, ins, scratch=(), flops=0, moved=0):
    return pl.pallas_call(
        body,
        out_shape=outs,
        in_specs=ins,
        out_specs=[VMEM] * len(outs),
        scratch_shapes=list(scratch),
        compiler_params=pltpu.CompilerParams(vmem_limit_bytes=VMEM_LIMIT),
        cost_estimate=pl.CostEstimate(flops=flops, bytes_accessed=moved, transcendentals=0),
    )


def shape(dims, dtype):
    return jax.ShapeDtypeStruct(dims, dtype)


def silu(block):
    wide = block.astype(F32)
    return (wide / (1.0 + jnp.exp(-wide))).astype(BF16)


def head_cols(head):
    return pl.ds(pl.multiple_of(head * HD, HD), HD)


def states_kernel(place, k_ref, v_ref, *outs):
    per = outs[0].shape[0]
    for j, out in enumerate(outs):
        quarter = place[0] ^ j
        for i in range(per):
            cols = head_cols(quarter * per + i)
            out[i] = lax.dot_general(
                silu(k_ref[:, cols]), v_ref[:, cols], (((0,), (0,)), ((), ())), preferred_element_type=F32
            ).astype(BF16)


def intra_kernel(q_ref, k_ref, v_ref, intra, feat):
    rows = q_ref.shape[0]
    causal = lax.broadcasted_iota(jnp.int32, (rows, rows), 0) >= lax.broadcasted_iota(jnp.int32, (rows, rows), 1)
    for h in range(q_ref.shape[1] // HD):
        cols = slice(h * HD, (h + 1) * HD)
        fq = silu(q_ref[:, cols])
        feat[:, cols] = fq
        scores = lax.dot_general(
            fq, silu(k_ref[:, cols]), (((1,), (1,)), ((), ())), preferred_element_type=F32
        )
        scores = jnp.where(causal, scores, 0.0).astype(BF16)
        intra[:, cols] = jnp.dot(scores, v_ref[:, cols], preferred_element_type=F32)


def total_kernel(a0, a1, a2, a3, out):
    out[...] = ((a0[...].astype(F32) + a1[...].astype(F32)) + (a2[...].astype(F32) + a3[...].astype(F32))).astype(BF16)


def prefixes_kernel(steps, place, *refs):
    own, shifts, outs = refs[:PLANE], refs[PLANE:PLANE + steps], refs[PLANE + steps:]
    before = sum(ref[...].astype(F32) for ref in shifts)
    for j, out in enumerate(outs):
        total = before
        for i, ref in enumerate(own):
            total = total + jnp.where((place[0] ^ i) < (place[0] ^ j), ref[...].astype(F32), 0.0)
        out[...] = total.astype(BF16)


def norm_kernel(place, intra, feat, c0, c1, c2, c3, gain, normed):
    for j, state in enumerate((c0, c1, c2, c3)):
        per = state.shape[0]
        for i in range(per):
            cols = head_cols((place[0] ^ j) * per + i)
            mixed = intra[:, cols] + jnp.dot(feat[:, cols], state[i], preferred_element_type=F32)
            scale = lax.rsqrt(jnp.mean(mixed * mixed, axis=-1, keepdims=True) + 1e-06)
            normed[:, cols] = (mixed * scale * gain[:, cols]).astype(BF16)


def norm_send_kernel(place, intra, feat, c0, c1, c2, c3, gain, normed, to_x, to_y):
    norm_kernel(place, intra, feat, c0, c1, c2, c3, gain, normed)
    x, y = place[0] & 1, place[0] >> 1
    for t in range(4):
        slot = slice(t * HD, (t + 1) * HD)
        to_x[:, slot] = normed[:, head_cols(2 * t + (1 - x))]
        to_y[:, slot] = normed[:, head_cols(4 * (t // 2) + 2 * (1 - y) + t % 2)]


def load_weights(pieces, held, sems):
    copies = []
    for at, piece in enumerate(pieces):
        copies.append(pltpu.make_async_copy(piece, held.at[pl.ds(at * HD, HD)], sems.at[at]))
        copies[-1].start()
    return copies


def partner_kernel(place, *refs):
    wa, wb = refs[0:8], refs[8:16]
    x_own, x_other, y_own, y_other, out_a, out_b, held_a, held_b, left, got, sems = refs[16:]
    copies_a = load_weights(wa, held_a, sems.at[0])
    copies_b = load_weights(wb, held_b, sems.at[1])
    x, y, z, core = place[0] & 1, place[0] >> 1, place[1], place[2]
    for own, other, along, out, held, copies in (
        (x_own, x_other, y, out_a, held_a, copies_a),
        (y_own, y_other, x, out_b, held_b, copies_b),
    ):
        got[core] = own[...]
        got[1 - core] = other[...]
        for r in range(4):
            from_z = (z - r) & 3
            for t in range(2):
                at = 2 * (from_z & 1) + (along ^ t)
                left[:, (2 * r + t) * HD:(2 * r + t + 1) * HD] = got[from_z >> 1, :, head_cols(at)]
        for copy in copies:
            copy.wait()
        out[...] = jnp.dot(left[...], held[...], preferred_element_type=F32).astype(BF16)


def own_kernel(place, *refs):
    wa, wb = refs[0:8], refs[8:16]
    own, other, out, held_a, held_b, left, got, sems = refs[16:]
    copies_a = load_weights(wa, held_a, sems.at[0])
    copies_b = load_weights(wb, held_b, sems.at[1])
    x, y, z, core = place[0] & 1, place[0] >> 1, place[1], place[2]
    got[core] = own[...]
    got[1 - core] = other[...]
    half = held_a.shape[1]
    for first, held, copies in ((0, held_a, copies_a), (1, held_b, copies_b)):
        for r in range(4):
            from_z = (z - r) & 3
            for t in range(2):
                flip = (t << 1) if first == 0 else t
                at = 4 * (from_z & 1) + ((2 * y + x) ^ flip)
                left[:, (2 * r + t) * HD:(2 * r + t + 1) * HD] = got[from_z >> 1, :, head_cols(at)]
        for copy in copies:
            copy.wait()
        out[:, first * half:(first + 1) * half] = jnp.dot(left[...], held[...], preferred_element_type=F32)


def per_device(queries, keys, values, norm_gain, w_out):
    rows, feats = queries.shape
    heads = feats // HD
    blocks = lax.axis_size("seq")
    me, core = lax.axis_index("seq"), lax.axis_index("mp")
    position, level = me % PLANE, me // PLANE
    place = jnp.stack([position, level, core]).astype(jnp.int32)

    def partner(value, flip):
        return lax.ppermute(value, "seq", [(i, i ^ flip) for i in range(blocks)])

    def ring(value):
        return lax.ppermute(value, "seq", [(i, (i + PLANE) % blocks) for i in range(blocks)])

    def up(value, by):
        return lax.ppermute(value, "seq", [(i, i + by * PLANE) for i in range(blocks - by * PLANE)])

    def swap(value):
        return lax.ppermute(value, "mp", [(0, 1), (1, 0)])

    per = heads // PLANE
    quarter = shape((per, HD, HD), BF16)
    own = call(states_kernel, [quarter] * PLANE, [SMEM, VMEM, VMEM], flops=2 * rows * feats * HD)(place, keys, values)
    intra, feat = call(
        intra_kernel, [shape((rows, feats), F32), shape((rows, feats), BF16)], [VMEM] * 3, flops=4 * rows * rows * feats
    )(queries, keys, values)
    mine = [own[0]] + [partner(own[j], j) for j in range(1, PLANE)]
    (running,) = call(total_kernel, [quarter], [VMEM] * PLANE)(*mine)
    shifts, by = [], 1
    while by * PLANE < blocks:
        shifts.append(up(running, by))
        running = (running.astype(F32) + shifts[-1].astype(F32)).astype(BF16)
        by *= 2
    prefixes = call(
        functools.partial(prefixes_kernel, len(shifts)), [quarter] * PLANE, [SMEM] + [VMEM] * (PLANE + len(shifts))
    )(place, *mine, *shifts)
    states = [prefixes[0]] + [partner(prefixes[j], j) for j in range(1, PLANE)]
    gain = norm_gain.reshape(1, feats)
    normed_args = (place, intra, feat, *states, gain)

    if w_out.shape[0] != HD or blocks != 4 * PLANE:
        (normed,) = call(norm_kernel, [shape((rows, feats), BF16)], [SMEM] + [VMEM] * 7)(*normed_args)
        all_heads = lax.all_gather(normed, "mp", axis=1, tiled=True)
        weight = lax.all_gather(w_out, "seq", axis=0, tiled=True)
        return jnp.dot(all_heads, weight, preferred_element_type=F32).astype(BF16)

    cols = w_out.shape[1]
    half = cols // 2
    wa, wb = [], []
    a, b = w_out[:, :half], w_out[:, half:]
    for r in range(4):
        wa += [a, partner(a, 2)]
        wb += [b, partner(b, 1)]
        if r < 3:
            a, b = ring(a), ring(b)

    normed, to_x, to_y = call(
        norm_send_kernel,
        [shape((rows, feats), BF16)] + [shape((rows, feats // 2), BF16)] * 2,
        [SMEM] + [VMEM] * 7,
        flops=2 * rows * feats * HD,
    )(*normed_args)
    got_x, got_y = partner(to_x, 1), partner(to_y, 2)
    other = swap(normed)
    weights = [ANY] * 16
    flops = 2 * rows * cols * (feats)
    room = [pltpu.VMEM((8 * HD, half), BF16)] * 2 + [pltpu.VMEM((rows, feats), BF16)]
    sems = pltpu.SemaphoreType.DMA((2, 8))
    part_a, part_b = call(
        partner_kernel,
        [shape((rows, half), BF16)] * 2,
        [SMEM] + weights + [VMEM] * 4,
        room + [pltpu.VMEM((2, rows, feats // 2), BF16), sems],
        flops=flops,
    )(place, *wa, *wb, got_x, swap(got_x), got_y, swap(got_y))
    (mine_all,) = call(
        own_kernel,
        [shape((rows, cols), F32)],
        [SMEM] + weights + [VMEM] * 2,
        room + [pltpu.VMEM((2, rows, feats), BF16), sems],
        flops=flops,
    )(place, *wa, *wb, normed, other)
    theirs = jnp.concatenate([partner(part_a, 1), partner(part_b, 2)], axis=1)
    return (mine_all + theirs.astype(F32)).astype(BF16)


def solution(mesh):
    in_specs = (P("seq", "mp"), P("seq", "mp"), P("seq", "mp"), P("mp"), P("seq", "mp"))
    out_specs = P("seq", "mp")
    return jax.shard_map(
        per_device, mesh=mesh, in_specs=in_specs, out_specs=out_specs, check_vma=False
    )
```

```python
import functools

import jax
import jax.numpy as jnp
from jax import lax
from jax.experimental import pallas as pl
from jax.experimental.pallas import tpu as pltpu
from jax.sharding import PartitionSpec as P

HD = 128
PLANE = 4
F32, BF16 = jnp.float32, jnp.bfloat16
VMEM_LIMIT = 40 * 1024 * 1024

ANY = pl.BlockSpec(memory_space=pl.ANY)
VMEM = pl.BlockSpec(memory_space=pltpu.VMEM)
SMEM = pl.BlockSpec(memory_space=pltpu.SMEM)


def call(body, outs, ins, scratch=(), flops=0, moved=0):
    return pl.pallas_call(
        body,
        out_shape=outs,
        in_specs=ins,
        out_specs=[VMEM] * len(outs),
        scratch_shapes=list(scratch),
        compiler_params=pltpu.CompilerParams(vmem_limit_bytes=VMEM_LIMIT),
        cost_estimate=pl.CostEstimate(flops=flops, bytes_accessed=moved, transcendentals=0),
    )


def shape(dims, dtype):
    return jax.ShapeDtypeStruct(dims, dtype)


def silu(block):
    wide = block.astype(F32)
    return (wide / (1.0 + jnp.exp(-wide))).astype(BF16)


def head_cols(head):
    return pl.ds(pl.multiple_of(head * HD, HD), HD)


def states_kernel(place, k_ref, v_ref, *outs):
    per = outs[0].shape[0]
    for j, out in enumerate(outs):
        quarter = place[0] ^ j
        for i in range(per):
            cols = head_cols(quarter * per + i)
            out[i] = lax.dot_general(
                silu(k_ref[:, cols]), v_ref[:, cols], (((0,), (0,)), ((), ())), preferred_element_type=F32
            ).astype(BF16)


def intra_kernel(q_ref, k_ref, v_ref, intra, feat):
    rows = q_ref.shape[0]
    causal = lax.broadcasted_iota(jnp.int32, (rows, rows), 0) >= lax.broadcasted_iota(jnp.int32, (rows, rows), 1)
    for h in range(q_ref.shape[1] // HD):
        cols = slice(h * HD, (h + 1) * HD)
        fq = silu(q_ref[:, cols])
        feat[:, cols] = fq
        scores = lax.dot_general(
            fq, silu(k_ref[:, cols]), (((1,), (1,)), ((), ())), preferred_element_type=F32
        )
        scores = jnp.where(causal, scores, 0.0).astype(BF16)
        intra[:, cols] = jnp.dot(scores, v_ref[:, cols], preferred_element_type=F32)


def total_kernel(a0, a1, a2, a3, out):
    out[...] = ((a0[...].astype(F32) + a1[...].astype(F32)) + (a2[...].astype(F32) + a3[...].astype(F32))).astype(BF16)


def prefixes_kernel(steps, place, *refs):
    own, shifts, outs = refs[:PLANE], refs[PLANE:PLANE + steps], refs[PLANE + steps:]
    before = sum(ref[...].astype(F32) for ref in shifts)
    for j, out in enumerate(outs):
        total = before
        for i, ref in enumerate(own):
            total = total + jnp.where((place[0] ^ i) < (place[0] ^ j), ref[...].astype(F32), 0.0)
        out[...] = total.astype(BF16)


def norm_kernel(place, intra, feat, c0, c1, c2, c3, gain, normed):
    for j, state in enumerate((c0, c1, c2, c3)):
        per = state.shape[0]
        for i in range(per):
            cols = head_cols((place[0] ^ j) * per + i)
            mixed = intra[:, cols] + jnp.dot(feat[:, cols], state[i], preferred_element_type=F32)
            scale = lax.rsqrt(jnp.mean(mixed * mixed, axis=-1, keepdims=True) + 1e-06)
            normed[:, cols] = (mixed * scale * gain[:, cols]).astype(BF16)


def norm_send_kernel(place, intra, feat, c0, c1, c2, c3, gain, normed, to_x, to_y):
    norm_kernel(place, intra, feat, c0, c1, c2, c3, gain, normed)
    x, y = place[0] & 1, place[0] >> 1
    for t in range(4):
        slot = slice(t * HD, (t + 1) * HD)
        to_x[:, slot] = normed[:, head_cols(2 * t + (1 - x))]
        to_y[:, slot] = normed[:, head_cols(4 * (t // 2) + 2 * (1 - y) + t % 2)]


def head_at(place, r, t, way, flip):
    from_z = (place[1] + way * r) & 3
    return from_z >> 1, 4 * (from_z & 1) + (place[0] ^ (t * flip))


def sums(place, pieces, own, other, way, flip, thin):
    left = []
    for r in range(4):
        for t in range(2):
            core, head = head_at(place, r, t, way, flip)
            if thin:
                head = (head >> 1) if flip == 2 else 2 * (head >> 2) + (head & 1)
            cols = head_cols(head)
            left.append(jnp.where(core == place[2], own[:, cols], other[:, cols]))
    return jnp.dot(
        jnp.concatenate(left, axis=1), jnp.concatenate([p[...] for p in pieces], axis=0), preferred_element_type=F32
    )


def partner_kernel(way, flip, place, *refs):
    own, other, out = refs[8:]
    out[...] = sums(place, refs[:8], own, other, way, flip, True).astype(BF16)


def own_kernel(ways, place, *refs):
    own, other, out = refs[16:]
    cut = refs[0].shape[1]
    out[:, :cut] = sums(place, refs[:8], own, other, ways[0], 2, False)
    out[:, cut:] = sums(place, refs[8:16], own, other, ways[1], 1, False)


CUT = 8
ZD = 0
BD = 0
TIES = {'tot': '', 'z1': 'b1', 'z2': '', 'add': 'x0 y0', 'back': 'a2 y1', 'norm': 'b2', 'act': 'a3', 'act2': 'y2', 'act3': 'b3 x2'}


def tie(value, *others):
    return lax.optimization_barrier((value, *others))


def per_device(queries, keys, values, norm_gain, w_out):
    rows, feats = queries.shape
    heads = feats // HD
    blocks = lax.axis_size("seq")
    me, core = lax.axis_index("seq"), lax.axis_index("mp")
    position, level = me % PLANE, me // PLANE
    place = jnp.stack([position, level, core]).astype(jnp.int32)
    split = w_out.shape[0] == HD and blocks == 4 * PLANE

    def partner(value, flip):
        return lax.ppermute(value, "seq", [(i, i ^ flip) for i in range(blocks)])

    def ring(value, way=1):
        return lax.ppermute(value, "seq", [(i, (i + way * PLANE) % blocks) for i in range(blocks)])

    def up(value, by):
        return lax.ppermute(value, "seq", [(i, i + by * PLANE) for i in range(blocks - by * PLANE)])

    def swap(value):
        return lax.ppermute(value, "mp", [(0, 1), (1, 0)])

    cols = w_out.shape[1]
    half = cols * CUT // 16
    held = {"a0": w_out[:, :half], "b0": w_out[:, half:]}

    def piece(n):
        if n not in held:
            if n[0] in "ab":
                held[n] = ring(piece(n[0] + str(int(n[1]) - 1)), -1 if BD and n[0] == "b" else 1)
            else:
                held[n] = partner(piece({"x": "b", "y": "a"}[n[0]] + n[1]), {"x": 1, "y": 2}[n[0]])
        return held[n]

    def tied(value, name):
        names = TIES[name].split() if split else []
        if not names:
            return value
        value, *rest = tie(value, *[piece(n) for n in names])
        held.update(zip(names, rest))
        return value

    per = heads // PLANE
    quarter = shape((per, HD, HD), BF16)
    own = call(states_kernel, [quarter] * PLANE, [SMEM, VMEM, VMEM], flops=2 * rows * feats * HD)(place, keys, values)
    intra, feat = call(
        intra_kernel, [shape((rows, feats), F32), shape((rows, feats), BF16)], [VMEM] * 3, flops=4 * rows * rows * feats
    )(queries, keys, values)
    mine = [own[0]] + [partner(own[j], j) for j in range(1, PLANE)]
    mine[3] = tied(mine[3], "tot")
    (running,) = call(total_kernel, [quarter], [VMEM] * PLANE)(*mine)
    running = tied(running, "z1")
    if split and ZD:
        shifts = [up(running, by) for by in range(1, blocks // PLANE)]
    else:
        shifts, by = [], 1
        while by * PLANE < blocks:
            if by == 2:
                running = tied(running, "z2")
            shifts.append(up(running, by))
            running = (running.astype(F32) + shifts[-1].astype(F32)).astype(BF16)
            by *= 2
    shifts[-1] = tied(shifts[-1], "add")
    prefixes = call(
        functools.partial(prefixes_kernel, len(shifts)), [quarter] * PLANE, [SMEM] + [VMEM] * (PLANE + len(shifts))
    )(place, *mine, *shifts)
    prefixes = list(prefixes)
    prefixes[1] = tied(prefixes[1], "back")
    states = [prefixes[0]] + [partner(prefixes[j], j) for j in range(1, PLANE)]
    states[3] = tied(states[3], "norm")
    gain = norm_gain.reshape(1, feats)
    normed_args = (place, intra, feat, *states, gain)

    if not split:
        (normed,) = call(norm_kernel, [shape((rows, feats), BF16)], [SMEM] + [VMEM] * 7)(*normed_args)
        all_heads = lax.all_gather(normed, "mp", axis=1, tiled=True)
        weight = lax.all_gather(w_out, "seq", axis=0, tiled=True)
        return jnp.dot(all_heads, weight, preferred_element_type=F32).astype(BF16)

    normed, to_x, to_y = call(
        norm_send_kernel,
        [shape((rows, feats), BF16)] + [shape((rows, feats // 2), BF16)] * 2,
        [SMEM] + [VMEM] * 7,
        flops=2 * rows * feats * HD,
    )(*normed_args)
    if TIES["act"]:
        to_x, to_y = tie(to_x, to_y)
    to_x = tied(to_x, "act")
    got_x, got_y = partner(to_x, 1), partner(to_y, 2)
    got_x = tied(got_x, "act2")
    got_y = tied(got_y, "act3")
    wa, wb = [], []
    for r in range(4):
        wa += [piece("a%d" % r), piece("y%d" % r)]
        wb += [piece("b%d" % r), piece("x%d" % r)]
    other = swap(normed)
    ways = (-1, 1 if BD else -1)
    parts = []
    for way, flip, pieces, got in ((ways[0], 2, wa, got_x), (ways[1], 1, wb, got_y)):
        width = pieces[0].shape[1]
        (part,) = call(
            functools.partial(partner_kernel, way, flip),
            [shape((rows, width), BF16)],
            [SMEM] + [VMEM] * 10,
            flops=rows * feats * width * 2,
        )(place, *pieces, got, swap(got))
        parts.append(partner(part, 3 - flip))
    (mine_all,) = call(
        functools.partial(own_kernel, ways),
        [shape((rows, cols), F32)],
        [SMEM] + [VMEM] * 18,
        flops=rows * feats * cols * 2,
    )(place, *wa, *wb, normed, other)
    theirs = jnp.concatenate(parts, axis=1)
    return (mine_all + theirs.astype(F32)).astype(BF16)


def solution(mesh):
    in_specs = (P("seq", "mp"), P("seq", "mp"), P("seq", "mp"), P("mp"), P("seq", "mp"))
    out_specs = P("seq", "mp")
    return jax.shard_map(
        per_device, mesh=mesh, in_specs=in_specs, out_specs=out_specs, check_vma=False
    )
```

```python
import functools

import jax
import jax.numpy as jnp
from jax import lax
from jax.experimental import pallas as pl
from jax.experimental.pallas import tpu as pltpu
from jax.sharding import PartitionSpec as P

HD = 128
PLANE = 4
F32, BF16 = jnp.float32, jnp.bfloat16
VMEM_LIMIT = 40 * 1024 * 1024

ANY = pl.BlockSpec(memory_space=pl.ANY)
VMEM = pl.BlockSpec(memory_space=pltpu.VMEM)
SMEM = pl.BlockSpec(memory_space=pltpu.SMEM)


def call(body, outs, ins, scratch=(), flops=0, moved=0):
    return pl.pallas_call(
        body,
        out_shape=outs,
        in_specs=ins,
        out_specs=[VMEM] * len(outs),
        scratch_shapes=list(scratch),
        compiler_params=pltpu.CompilerParams(vmem_limit_bytes=VMEM_LIMIT),
        cost_estimate=pl.CostEstimate(flops=flops, bytes_accessed=moved, transcendentals=0),
    )


def shape(dims, dtype):
    return jax.ShapeDtypeStruct(dims, dtype)


def silu(block):
    wide = block.astype(F32)
    return (wide / (1.0 + jnp.exp(-wide))).astype(BF16)


def head_cols(head):
    return pl.ds(pl.multiple_of(head * HD, HD), HD)


def states_kernel(place, k_ref, v_ref, *outs):
    per = outs[0].shape[0]
    for j, out in enumerate(outs):
        quarter = place[0] ^ j
        for i in range(per):
            cols = head_cols(quarter * per + i)
            out[i] = lax.dot_general(
                silu(k_ref[:, cols]), v_ref[:, cols], (((0,), (0,)), ((), ())), preferred_element_type=F32
            ).astype(BF16)


def intra_kernel(q_ref, k_ref, v_ref, intra, feat):
    rows = q_ref.shape[0]
    causal = lax.broadcasted_iota(jnp.int32, (rows, rows), 0) >= lax.broadcasted_iota(jnp.int32, (rows, rows), 1)
    for h in range(q_ref.shape[1] // HD):
        cols = slice(h * HD, (h + 1) * HD)
        fq = silu(q_ref[:, cols])
        feat[:, cols] = fq
        scores = lax.dot_general(
            fq, silu(k_ref[:, cols]), (((1,), (1,)), ((), ())), preferred_element_type=F32
        )
        scores = jnp.where(causal, scores, 0.0).astype(BF16)
        intra[:, cols] = jnp.dot(scores, v_ref[:, cols], preferred_element_type=F32)


def total_kernel(a0, a1, a2, a3, out):
    out[...] = ((a0[...].astype(F32) + a1[...].astype(F32)) + (a2[...].astype(F32) + a3[...].astype(F32))).astype(BF16)


def prefixes_kernel(steps, place, *refs):
    own, shifts, outs = refs[:PLANE], refs[PLANE:PLANE + steps], refs[PLANE + steps:]
    before = sum(ref[...].astype(F32) for ref in shifts)
    for j, out in enumerate(outs):
        total = before
        for i, ref in enumerate(own):
            total = total + jnp.where((place[0] ^ i) < (place[0] ^ j), ref[...].astype(F32), 0.0)
        out[...] = total.astype(BF16)


def norm_kernel(place, intra, feat, c0, c1, c2, c3, gain, normed):
    for j, state in enumerate((c0, c1, c2, c3)):
        per = state.shape[0]
        for i in range(per):
            cols = head_cols((place[0] ^ j) * per + i)
            mixed = intra[:, cols] + jnp.dot(feat[:, cols], state[i], preferred_element_type=F32)
            scale = lax.rsqrt(jnp.mean(mixed * mixed, axis=-1, keepdims=True) + 1e-06)
            normed[:, cols] = (mixed * scale * gain[:, cols]).astype(BF16)


def norm_send_kernel(place, intra, feat, c0, c1, c2, c3, gain, normed, to_x, to_y):
    norm_kernel(place, intra, feat, c0, c1, c2, c3, gain, normed)
    x, y = place[0] & 1, place[0] >> 1
    for t in range(4):
        slot = slice(t * HD, (t + 1) * HD)
        to_x[:, slot] = normed[:, head_cols(2 * t + (1 - x))]
        to_y[:, slot] = normed[:, head_cols(4 * (t // 2) + 2 * (1 - y) + t % 2)]


def head_at(place, r, t, way, flip):
    from_z = (place[1] + way * r) & 3
    return from_z >> 1, 4 * (from_z & 1) + (place[0] ^ (t * flip))


def sums(place, pieces, own, other, way, flip, thin):
    left = []
    for r in range(4):
        for t in range(2):
            core, head = head_at(place, r, t, way, flip)
            if thin:
                head = (head >> 1) if flip == 2 else 2 * (head >> 2) + (head & 1)
            cols = head_cols(head)
            left.append(jnp.where(core == place[2], own[:, cols], other[:, cols]))
    return jnp.dot(
        jnp.concatenate(left, axis=1), jnp.concatenate([p[...] for p in pieces], axis=0), preferred_element_type=F32
    )


def partner_kernel(way, flip, place, *refs):
    own, other, out = refs[8:]
    out[...] = sums(place, refs[:8], own, other, way, flip, True).astype(BF16)


def own_kernel(ways, place, *refs):
    own, other, out = refs[16:]
    cut = refs[0].shape[1]
    out[:, :cut] = sums(place, refs[:8], own, other, ways[0], 2, False)
    out[:, cut:] = sums(place, refs[8:16], own, other, ways[1], 1, False)


def cut_kernel(block, first, second, sems):
    width = first.shape[1]
    copies = [
        pltpu.make_async_copy(block.at[:, pl.ds(0, width)], first, sems.at[0]),
        pltpu.make_async_copy(block.at[:, pl.ds(width, second.shape[1])], second, sems.at[1]),
    ]
    for copy in copies:
        copy.start()
    for copy in copies:
        copy.wait()


def finish_kernel(at, mine, part, *refs):
    out, held, sems = refs[-3:]
    rows, width = part.shape
    step = rows // 4
    copies = []
    for i in range(4):
        these = slice(i * step, (i + 1) * step)
        held[these] = (mine[these, at:at + width] + part[these].astype(F32)).astype(BF16)
        copies.append(
            pltpu.make_async_copy(
                held.at[pl.ds(i * step, step)], out.at[pl.ds(i * step, step), pl.ds(at, width)], sems.at[i]
            )
        )
        copies[-1].start()
    for copy in copies:
        copy.wait()


def finish(mine, part, at, result):
    return pl.pallas_call(
        functools.partial(finish_kernel, at),
        out_shape=shape(mine.shape, BF16),
        in_specs=[VMEM] * 2 + ([ANY] if result is not None else []),
        out_specs=ANY,
        scratch_shapes=[pltpu.VMEM(part.shape, BF16), pltpu.SemaphoreType.DMA((4,))],
        input_output_aliases={2: 0} if result is not None else {},
        compiler_params=pltpu.CompilerParams(vmem_limit_bytes=VMEM_LIMIT),
    )(*([mine, part] + ([result] if result is not None else [])))


CUT = 8
ZD = 0
BD = 0
TIES = {'tot': '', 'z1': 'y0', 'z2': '', 'add': 'x0', 'back': 'a2 x1 y1', 'norm': '', 'act': 'a3', 'act2': 'y3', 'act3': 'b3'}


def tie(value, *others):
    return lax.optimization_barrier((value, *others))


def per_device(queries, keys, values, norm_gain, w_out):
    rows, feats = queries.shape
    heads = feats // HD
    blocks = lax.axis_size("seq")
    me, core = lax.axis_index("seq"), lax.axis_index("mp")
    position, level = me % PLANE, me // PLANE
    place = jnp.stack([position, level, core]).astype(jnp.int32)
    split = w_out.shape[0] == HD and blocks == 4 * PLANE

    def partner(value, flip):
        return lax.ppermute(value, "seq", [(i, i ^ flip) for i in range(blocks)])

    def ring(value, way=1):
        return lax.ppermute(value, "seq", [(i, (i + way * PLANE) % blocks) for i in range(blocks)])

    def up(value, by):
        return lax.ppermute(value, "seq", [(i, i + by * PLANE) for i in range(blocks - by * PLANE)])

    def swap(value):
        return lax.ppermute(value, "mp", [(0, 1), (1, 0)])

    cols = w_out.shape[1]
    half = cols * CUT // 16
    held = {"a0": w_out[:, :half], "b0": w_out[:, half:]}

    def piece(n):
        if n not in held:
            if n == "r1":
                held[n] = ring(w_out)
            elif n in ("a1", "b1"):
                held["a1"], held["b1"] = call(
                    cut_kernel,
                    [shape((HD, half), BF16), shape((HD, cols - half), BF16)],
                    [ANY],
                    [pltpu.SemaphoreType.DMA((2,))],
                )(piece("r1"))
            elif n[0] in "ab":
                held[n] = ring(piece(n[0] + str(int(n[1]) - 1)), -1 if BD and n[0] == "b" else 1)
            else:
                held[n] = partner(piece({"x": "b", "y": "a"}[n[0]] + n[1]), {"x": 1, "y": 2}[n[0]])
        return held[n]

    def tied(value, name):
        names = TIES[name].split() if split else []
        if not names:
            return value
        value, *rest = tie(value, *[piece(n) for n in names])
        held.update(zip(names, rest))
        return value

    per = heads // PLANE
    quarter = shape((per, HD, HD), BF16)
    own = call(states_kernel, [quarter] * PLANE, [SMEM, VMEM, VMEM], flops=2 * rows * feats * HD)(place, keys, values)
    intra, feat = call(
        intra_kernel, [shape((rows, feats), F32), shape((rows, feats), BF16)], [VMEM] * 3, flops=4 * rows * rows * feats
    )(queries, keys, values)
    mine = [own[0]] + [partner(own[j], j) for j in range(1, PLANE)]
    mine[3] = tied(mine[3], "tot")
    (running,) = call(total_kernel, [quarter], [VMEM] * PLANE)(*mine)
    running = tied(running, "z1")
    if split and ZD:
        shifts = [up(running, by) for by in range(1, blocks // PLANE)]
    else:
        shifts, by = [], 1
        while by * PLANE < blocks:
            if by == 2:
                running = tied(running, "z2")
            shifts.append(up(running, by))
            running = (running.astype(F32) + shifts[-1].astype(F32)).astype(BF16)
            by *= 2
    shifts[-1] = tied(shifts[-1], "add")
    prefixes = call(
        functools.partial(prefixes_kernel, len(shifts)), [quarter] * PLANE, [SMEM] + [VMEM] * (PLANE + len(shifts))
    )(place, *mine, *shifts)
    prefixes = list(prefixes)
    prefixes[1] = tied(prefixes[1], "back")
    states = [prefixes[0]] + [partner(prefixes[j], j) for j in range(1, PLANE)]
    states[3] = tied(states[3], "norm")
    gain = norm_gain.reshape(1, feats)
    normed_args = (place, intra, feat, *states, gain)

    if not split:
        (normed,) = call(norm_kernel, [shape((rows, feats), BF16)], [SMEM] + [VMEM] * 7)(*normed_args)
        all_heads = lax.all_gather(normed, "mp", axis=1, tiled=True)
        weight = lax.all_gather(w_out, "seq", axis=0, tiled=True)
        return jnp.dot(all_heads, weight, preferred_element_type=F32).astype(BF16)

    normed, to_x, to_y = call(
        norm_send_kernel,
        [shape((rows, feats), BF16)] + [shape((rows, feats // 2), BF16)] * 2,
        [SMEM] + [VMEM] * 7,
        flops=2 * rows * feats * HD,
    )(*normed_args)
    if TIES["act"]:
        to_x, to_y = tie(to_x, to_y)
    to_x = tied(to_x, "act")
    got_x, got_y = partner(to_x, 1), partner(to_y, 2)
    got_x = tied(got_x, "act2")
    got_y = tied(got_y, "act3")
    wa, wb = [], []
    for r in range(4):
        wa += [piece("a%d" % r), piece("y%d" % r)]
        wb += [piece("b%d" % r), piece("x%d" % r)]
    other = swap(normed)
    ways = (-1, 1 if BD else -1)
    parts = []
    for way, flip, pieces, got in ((ways[0], 2, wa, got_x), (ways[1], 1, wb, got_y)):
        width = pieces[0].shape[1]
        (part,) = call(
            functools.partial(partner_kernel, way, flip),
            [shape((rows, width), BF16)],
            [SMEM] + [VMEM] * 10,
            flops=rows * feats * width * 2,
        )(place, *pieces, got, swap(got))
        parts.append(partner(part, 3 - flip))
    (mine_all,) = call(
        functools.partial(own_kernel, ways),
        [shape((rows, cols), F32)],
        [SMEM] + [VMEM] * 18,
        flops=rows * feats * cols * 2,
    )(place, *wa, *wb, normed, other)
    result = None
    for at, part in ((half, parts[1]), (0, parts[0])):
        result = finish(mine_all, part, at, result)
    return result


def solution(mesh):
    in_specs = (P("seq", "mp"), P("seq", "mp"), P("seq", "mp"), P("mp"), P("seq", "mp"))
    out_specs = P("seq", "mp")
    return jax.shard_map(
        per_device, mesh=mesh, in_specs=in_specs, out_specs=out_specs, check_vma=False
    )
```

```python
import functools

import jax
import jax.numpy as jnp
from jax import lax
from jax.experimental import pallas as pl
from jax.experimental.pallas import tpu as pltpu
from jax.sharding import PartitionSpec as P

HD = 128
PLANE = 4
F32, BF16 = jnp.float32, jnp.bfloat16
VMEM_LIMIT = 40 * 1024 * 1024

COST = 0
PER_US = 1.15e9

ANY = pl.BlockSpec(memory_space=pl.ANY)
VMEM = pl.BlockSpec(memory_space=pltpu.VMEM)


def call(body, outs, ins, scratch=(), flops=0, moved=0, us=0.0):
    return pl.pallas_call(
        body,
        out_shape=outs,
        in_specs=ins,
        out_specs=[VMEM] * len(outs),
        scratch_shapes=list(scratch),
        compiler_params=pltpu.CompilerParams(vmem_limit_bytes=VMEM_LIMIT),
        cost_estimate=pl.CostEstimate(flops=int(us * PER_US) if us and (COST or not flops) else flops, bytes_accessed=moved, transcendentals=0),
    )


def shape(dims, dtype):
    return jax.ShapeDtypeStruct(dims, dtype)


def spot():
    me = lax.axis_index("seq")
    return me % PLANE, me // PLANE, lax.axis_index("mp")


def silu(block):
    wide = block.astype(F32)
    return (wide / (1.0 + jnp.exp(-wide))).astype(BF16)


def head_cols(head):
    return pl.ds(pl.multiple_of(head * HD, HD), HD)


def states_kernel(k_ref, v_ref, *outs):
    place = spot()
    per = outs[0].shape[0]
    for j, out in enumerate(outs):
        quarter = place[0] ^ j
        for i in range(per):
            cols = head_cols(quarter * per + i)
            out[i] = lax.dot_general(
                silu(k_ref[:, cols]), v_ref[:, cols], (((0,), (0,)), ((), ())), preferred_element_type=F32
            ).astype(BF16)


def intra_kernel(q_ref, k_ref, v_ref, intra, feat):
    rows = q_ref.shape[0]
    causal = lax.broadcasted_iota(jnp.int32, (rows, rows), 0) >= lax.broadcasted_iota(jnp.int32, (rows, rows), 1)
    for h in range(q_ref.shape[1] // HD):
        cols = slice(h * HD, (h + 1) * HD)
        fq = silu(q_ref[:, cols])
        feat[:, cols] = fq
        scores = lax.dot_general(
            fq, silu(k_ref[:, cols]), (((1,), (1,)), ((), ())), preferred_element_type=F32
        )
        scores = jnp.where(causal, scores, 0.0).astype(BF16)
        intra[:, cols] = jnp.dot(scores, v_ref[:, cols], preferred_element_type=F32)


def total_kernel(a0, a1, a2, a3, out):
    out[...] = ((a0[...].astype(F32) + a1[...].astype(F32)) + (a2[...].astype(F32) + a3[...].astype(F32))).astype(BF16)


def prefixes_kernel(steps, *refs):
    place = spot()
    own, shifts, outs = refs[:PLANE], refs[PLANE:PLANE + steps], refs[PLANE + steps:]
    before = sum(ref[...].astype(F32) for ref in shifts)
    for j, out in enumerate(outs):
        total = before
        for i, ref in enumerate(own):
            total = total + jnp.where((place[0] ^ i) < (place[0] ^ j), ref[...].astype(F32), 0.0)
        out[...] = total.astype(BF16)


def norm_kernel(intra, feat, c0, c1, c2, c3, gain, normed):
    place = spot()
    for j, state in enumerate((c0, c1, c2, c3)):
        per = state.shape[0]
        for i in range(per):
            cols = head_cols((place[0] ^ j) * per + i)
            mixed = intra[:, cols] + jnp.dot(feat[:, cols], state[i], preferred_element_type=F32)
            scale = lax.rsqrt(jnp.mean(mixed * mixed, axis=-1, keepdims=True) + 1e-06)
            normed[:, cols] = (mixed * scale * gain[:, cols]).astype(BF16)


def norm_send_kernel(intra, feat, c0, c1, c2, c3, gain, normed, to_x, to_y):
    place = spot()
    norm_kernel(intra, feat, c0, c1, c2, c3, gain, normed)
    x, y = place[0] & 1, place[0] >> 1
    for t in range(4):
        slot = slice(t * HD, (t + 1) * HD)
        to_x[:, slot] = normed[:, head_cols(2 * t + (1 - x))]
        to_y[:, slot] = normed[:, head_cols(4 * (t // 2) + 2 * (1 - y) + t % 2)]


def head_at(place, r, t, way, flip):
    from_z = (place[1] + way * r) & 3
    return from_z >> 1, 4 * (from_z & 1) + (place[0] ^ (t * flip))


def sums(place, pieces, got, way, flip, thin):
    left = []
    for r in range(4):
        for t in range(2):
            core, head = head_at(place, r, t, way, flip)
            if thin:
                head = (head >> 1) if flip == 2 else 2 * (head >> 2) + (head & 1)
            cols = head_cols(head)
            left.append(got[core, :, cols])
    return jnp.dot(
        jnp.concatenate(left, axis=1), jnp.concatenate([p[...] for p in pieces], axis=0), preferred_element_type=F32
    )


def partner_kernel(way, flip, *refs):
    place = spot()
    own, other, out, got = refs[8:]
    got[place[2]] = own[...]
    got[1 - place[2]] = other[...]
    out[...] = sums(place, refs[:8], got, way, flip, True).astype(BF16)


def own_kernel(ways, *refs):
    place = spot()
    own, other, out, got = refs[16:]
    got[place[2]] = own[...]
    got[1 - place[2]] = other[...]
    cut = refs[0].shape[1]
    out[:, :cut] = sums(place, refs[:8], got, ways[0], 2, False)
    out[:, cut:] = sums(place, refs[8:16], got, ways[1], 1, False)


def cut_kernel(block, first, second, sems):
    width = first.shape[1]
    copies = [
        pltpu.make_async_copy(block.at[:, pl.ds(0, width)], first, sems.at[0]),
        pltpu.make_async_copy(block.at[:, pl.ds(width, second.shape[1])], second, sems.at[1]),
    ]
    for copy in copies:
        copy.start()
    for copy in copies:
        copy.wait()


def finish_kernel(at, mine, part, *refs):
    out, held, sems = refs[-3:]
    rows, width = part.shape
    step = rows // 4
    copies = []
    for i in range(4):
        these = slice(i * step, (i + 1) * step)
        held[these] = (mine[these, at:at + width] + part[these].astype(F32)).astype(BF16)
        copies.append(
            pltpu.make_async_copy(
                held.at[pl.ds(i * step, step)], out.at[pl.ds(i * step, step), pl.ds(at, width)], sems.at[i]
            )
        )
        copies[-1].start()
    for copy in copies:
        copy.wait()


def finish(mine, part, at, result):
    return pl.pallas_call(
        functools.partial(finish_kernel, at),
        out_shape=shape(mine.shape, BF16),
        in_specs=[VMEM] * 2 + ([ANY] if result is not None else []),
        out_specs=ANY,
        scratch_shapes=[pltpu.VMEM(part.shape, BF16), pltpu.SemaphoreType.DMA((4,))],
        input_output_aliases={2: 0} if result is not None else {},
        compiler_params=pltpu.CompilerParams(vmem_limit_bytes=VMEM_LIMIT),
    )(*([mine, part] + ([result] if result is not None else [])))


CUT = 8
ZD = 0
DN = 0
CUT_US = 0
ORD = 0
TIES = {'tot': '', 'z1': 'y0', 'z2': '', 'add': 'a2 x0', 'back': 'x1', 'norm': 'y1', 'act': '', 'act2': 'a3 x2 y3', 'act3': 'b3'}


def tie(value, *others):
    return lax.optimization_barrier((value, *others))


def per_device(queries, keys, values, norm_gain, w_out):
    rows, feats = queries.shape
    heads = feats // HD
    blocks = lax.axis_size("seq")
    split = w_out.shape[0] == HD and blocks == 4 * PLANE

    def partner(value, flip):
        return lax.ppermute(value, "seq", [(i, i ^ flip) for i in range(blocks)])

    def ring(value, way=1):
        return lax.ppermute(value, "seq", [(i, (i + way * PLANE) % blocks) for i in range(blocks)])

    def up(value, by):
        return lax.ppermute(value, "seq", [(i, i + by * PLANE) for i in range(blocks - by * PLANE)])

    def swap(value):
        return lax.ppermute(value, "mp", [(0, 1), (1, 0)])

    cols = w_out.shape[1]
    half = cols * CUT // 16
    def cut(block, us=0.0):
        return call(
            cut_kernel,
            [shape((HD, half), BF16), shape((HD, cols - half), BF16)],
            [ANY],
            [pltpu.SemaphoreType.DMA((2,))],
            us=us,
        )(block)

    held = {}
    early_keys = keys
    if split:
        held["a0"], held["b0"] = cut(w_out, CUT_US)
        if CUT_US:
            early_keys, held["a0"] = tie(keys, held["a0"])

    def piece(n):
        if n not in held:
            if n == "r1":
                held[n] = ring(w_out)
            elif n in ("a1", "b1"):
                held["a1"], held["b1"] = cut(piece("r1"))
            elif n[0] in "ab":
                if DN and n[1] == "3":
                    held[n] = ring(piece(n[0] + "0"), -1)
                else:
                    held[n] = ring(piece(n[0] + str(int(n[1]) - 1)))
            else:
                held[n] = partner(piece({"x": "b", "y": "a"}[n[0]] + n[1]), {"x": 1, "y": 2}[n[0]])
        return held[n]

    def tied(value, name):
        names = TIES[name].split() if split else []
        if not names:
            return value
        value, *rest = tie(value, *[piece(n) for n in names])
        held.update(zip(names, rest))
        return value

    per = heads // PLANE
    quarter = shape((per, HD, HD), BF16)
    own = call(states_kernel, [quarter] * PLANE, [VMEM, VMEM], flops=2 * rows * feats * HD, us=1.1)(
        early_keys, values
    )
    intra, feat = call(
        intra_kernel, [shape((rows, feats), F32), shape((rows, feats), BF16)], [VMEM] * 3, flops=4 * rows * rows * feats, us=1.0
    )(queries, keys, values)
    mine = [own[0]] + [partner(own[j], j) for j in range(1, PLANE)]
    mine[3] = tied(mine[3], "tot")
    (running,) = call(total_kernel, [quarter], [VMEM] * PLANE)(*mine)
    running = tied(running, "z1")
    if split and ZD:
        shifts = [up(running, by) for by in range(1, blocks // PLANE)]
    else:
        shifts, by = [], 1
        while by * PLANE < blocks:
            if by == 2:
                running = tied(running, "z2")
            shifts.append(up(running, by))
            running = (running.astype(F32) + shifts[-1].astype(F32)).astype(BF16)
            by *= 2
    shifts[-1] = tied(shifts[-1], "add")
    prefixes = call(
        functools.partial(prefixes_kernel, len(shifts)), [quarter] * PLANE, [VMEM] * (PLANE + len(shifts)), flops=1
    )(*mine, *shifts)
    prefixes = list(prefixes)
    prefixes[1] = tied(prefixes[1], "back")
    states = [prefixes[0]] + [partner(prefixes[j], j) for j in range(1, PLANE)]
    states[3] = tied(states[3], "norm")
    gain = norm_gain.reshape(1, feats)
    normed_args = (intra, feat, *states, gain)

    if not split:
        (normed,) = call(norm_kernel, [shape((rows, feats), BF16)], [VMEM] * 7)(*normed_args)
        all_heads = lax.all_gather(normed, "mp", axis=1, tiled=True)
        weight = lax.all_gather(w_out, "seq", axis=0, tiled=True)
        return jnp.dot(all_heads, weight, preferred_element_type=F32).astype(BF16)

    normed, to_x, to_y = call(
        norm_send_kernel,
        [shape((rows, feats), BF16)] + [shape((rows, feats // 2), BF16)] * 2,
        [VMEM] * 7,
        flops=2 * rows * feats * HD,
        us=1.2,
    )(*normed_args)
    if TIES["act"]:
        to_x, to_y = tie(to_x, to_y)
    to_x = tied(to_x, "act")
    got_x, got_y = partner(to_x, 1), partner(to_y, 2)
    got_x = tied(got_x, "act2")
    got_y = tied(got_y, "act3")
    wa, wb = [], []
    for r in range(4):
        wa += [piece("a%d" % r), piece("y%d" % r)]
        wb += [piece("b%d" % r), piece("x%d" % r)]
    other = swap(normed)
    ways = (-1, -1)
    swapped = [swap(got_x), swap(got_y)]
    parts = [None, None]
    turns = [(0, 2, wa, got_x), (1, 1, wb, got_y)]
    for at, flip, pieces, got in turns[::-1] if ORD == 2 else turns:
        width = pieces[0].shape[1]
        (part,) = call(
            functools.partial(partner_kernel, ways[at], flip),
            [shape((rows, width), BF16)],
            [VMEM] * 10,
            [pltpu.VMEM((2, rows, feats // 2), BF16)],
            flops=rows * feats * width * 2,
            us=1.3,
        )(*pieces, got, swapped[at])
        if ORD and parts[1 - at] is None:
            part, swapped[1 - at] = tie(part, swapped[1 - at])
        parts[at] = partner(part, 3 - flip)
    (mine_all,) = call(
        functools.partial(own_kernel, ways),
        [shape((rows, cols), F32)],
        [VMEM] * 18,
        [pltpu.VMEM((2, rows, feats), BF16)],
        flops=rows * feats * cols * 2,
        us=2.0,
    )(*wa, *wb, normed, other)
    result = None
    for at, part in ((0, parts[0]), (half, parts[1]))[:: 1 if ORD == 1 else -1]:
        result = finish(mine_all, part, at, result)
    return result


def solution(mesh):
    in_specs = (P("seq", "mp"), P("seq", "mp"), P("seq", "mp"), P("mp"), P("seq", "mp"))
    out_specs = P("seq", "mp")
    return jax.shard_map(
        per_device, mesh=mesh, in_specs=in_specs, out_specs=out_specs, check_vma=False
    )
```

```python
import functools

import jax
import jax.numpy as jnp
from jax import lax
from jax.experimental import pallas as pl
from jax.experimental.pallas import tpu as pltpu
from jax.sharding import PartitionSpec as P

HD = 128
PLANE = 4
F32, BF16 = jnp.float32, jnp.bfloat16
VMEM_LIMIT = 40 * 1024 * 1024

ANY = pl.BlockSpec(memory_space=pl.ANY)
VMEM = pl.BlockSpec(memory_space=pltpu.VMEM)


def call(body, outs, ins, scratch=(), flops=0):
    return pl.pallas_call(
        body,
        out_shape=outs,
        in_specs=ins,
        out_specs=[VMEM] * len(outs),
        scratch_shapes=list(scratch),
        compiler_params=pltpu.CompilerParams(vmem_limit_bytes=VMEM_LIMIT),
        cost_estimate=pl.CostEstimate(flops=flops, bytes_accessed=0, transcendentals=0),
    )


def shape(dims, dtype):
    return jax.ShapeDtypeStruct(dims, dtype)


def spot():
    me = lax.axis_index("seq")
    return me % PLANE, me // PLANE, lax.axis_index("mp")


def silu(block):
    wide = block.astype(F32)
    return (wide / (1.0 + jnp.exp(-wide))).astype(BF16)


def head_cols(head):
    return pl.ds(pl.multiple_of(head * HD, HD), HD)


def states_kernel(k_ref, v_ref, *outs):
    place = spot()
    per = outs[0].shape[0]
    for j, out in enumerate(outs):
        quarter = place[0] ^ j
        for i in range(per):
            cols = head_cols(quarter * per + i)
            out[i] = lax.dot_general(
                silu(k_ref[:, cols]), v_ref[:, cols], (((0,), (0,)), ((), ())), preferred_element_type=F32
            ).astype(BF16)


def intra_kernel(q_ref, k_ref, v_ref, intra, feat):
    rows = q_ref.shape[0]
    causal = lax.broadcasted_iota(jnp.int32, (rows, rows), 0) >= lax.broadcasted_iota(jnp.int32, (rows, rows), 1)
    for h in range(q_ref.shape[1] // HD):
        cols = slice(h * HD, (h + 1) * HD)
        fq = silu(q_ref[:, cols])
        feat[:, cols] = fq
        scores = lax.dot_general(
            fq, silu(k_ref[:, cols]), (((1,), (1,)), ((), ())), preferred_element_type=F32
        )
        scores = jnp.where(causal, scores, 0.0).astype(BF16)
        intra[:, cols] = jnp.dot(scores, v_ref[:, cols], preferred_element_type=F32)


def total_kernel(a0, a1, a2, a3, out):
    out[...] = ((a0[...].astype(F32) + a1[...].astype(F32)) + (a2[...].astype(F32) + a3[...].astype(F32))).astype(BF16)


def prefixes_kernel(steps, *refs):
    place = spot()
    own, shifts, outs = refs[:PLANE], refs[PLANE:PLANE + steps], refs[PLANE + steps:]
    before = sum(ref[...].astype(F32) for ref in shifts)
    for j, out in enumerate(outs):
        total = before
        for i, ref in enumerate(own):
            total = total + jnp.where((place[0] ^ i) < (place[0] ^ j), ref[...].astype(F32), 0.0)
        out[...] = total.astype(BF16)


def norm_kernel(intra, feat, c0, c1, c2, c3, gain, normed):
    place = spot()
    for j, state in enumerate((c0, c1, c2, c3)):
        per = state.shape[0]
        for i in range(per):
            cols = head_cols((place[0] ^ j) * per + i)
            mixed = intra[:, cols] + jnp.dot(feat[:, cols], state[i], preferred_element_type=F32)
            scale = lax.rsqrt(jnp.mean(mixed * mixed, axis=-1, keepdims=True) + 1e-06)
            normed[:, cols] = (mixed * scale * gain[:, cols]).astype(BF16)


def norm_send_kernel(intra, feat, c0, c1, c2, c3, gain, normed, to_x, to_y):
    place = spot()
    norm_kernel(intra, feat, c0, c1, c2, c3, gain, normed)
    x, y = place[0] & 1, place[0] >> 1
    for t in range(4):
        slot = slice(t * HD, (t + 1) * HD)
        to_x[:, slot] = normed[:, head_cols(2 * t + (1 - x))]
        to_y[:, slot] = normed[:, head_cols(4 * (t // 2) + 2 * (1 - y) + t % 2)]


def head_at(place, r, t, flip):
    from_z = (place[1] - r) & 3
    return from_z >> 1, 4 * (from_z & 1) + (place[0] ^ (t * flip))


def sums(place, pieces, got, flip, thin):
    left = []
    for r in range(4):
        for t in range(2):
            core, head = head_at(place, r, t, flip)
            if thin:
                head = (head >> 1) if flip == 2 else 2 * (head >> 2) + (head & 1)
            cols = head_cols(head)
            left.append(got[core, :, cols])
    return jnp.dot(
        jnp.concatenate(left, axis=1), jnp.concatenate([p[...] for p in pieces], axis=0), preferred_element_type=F32
    )


def partner_kernel(flip, *refs):
    place = spot()
    own, other, out, got = refs[8:]
    got[place[2]] = own[...]
    got[1 - place[2]] = other[...]
    out[...] = sums(place, refs[:8], got, flip, True).astype(BF16)


def own_kernel(*refs):
    place = spot()
    own, other, out, got = refs[16:]
    got[place[2]] = own[...]
    got[1 - place[2]] = other[...]
    cut = refs[0].shape[1]
    out[:, :cut] = sums(place, refs[:8], got, 2, False)
    out[:, cut:] = sums(place, refs[8:16], got, 1, False)


def cut_kernel(block, first, second, sems):
    width = first.shape[1]
    copies = [
        pltpu.make_async_copy(block.at[:, pl.ds(0, width)], first, sems.at[0]),
        pltpu.make_async_copy(block.at[:, pl.ds(width, second.shape[1])], second, sems.at[1]),
    ]
    for copy in copies:
        copy.start()
    for copy in copies:
        copy.wait()


def finish_kernel(at, mine, part, *refs):
    out, held, sems = refs[-3:]
    rows, width = part.shape
    step = rows // 4
    copies = []
    for i in range(4):
        these = slice(i * step, (i + 1) * step)
        held[these] = (mine[these, at:at + width] + part[these].astype(F32)).astype(BF16)
        copies.append(
            pltpu.make_async_copy(
                held.at[pl.ds(i * step, step)], out.at[pl.ds(i * step, step), pl.ds(at, width)], sems.at[i]
            )
        )
        copies[-1].start()
    for copy in copies:
        copy.wait()


def finish(mine, part, at, result):
    return pl.pallas_call(
        functools.partial(finish_kernel, at),
        out_shape=shape(mine.shape, BF16),
        in_specs=[VMEM] * 2 + ([ANY] if result is not None else []),
        out_specs=ANY,
        scratch_shapes=[pltpu.VMEM(part.shape, BF16), pltpu.SemaphoreType.DMA((4,))],
        input_output_aliases={2: 0} if result is not None else {},
        compiler_params=pltpu.CompilerParams(vmem_limit_bytes=VMEM_LIMIT),
    )(*([mine, part] + ([result] if result is not None else [])))


DEADLINES = {'shift1': 'y0', 'shifted': 'a2 x0', 'back': 'x1', 'states': 'y1', 'got_x': 'a3 x2 y3', 'got_y': 'b3'}


def tie(value, *others):
    return lax.optimization_barrier((value, *others))


def per_device(queries, keys, values, norm_gain, w_out):
    rows, feats = queries.shape
    heads = feats // HD
    blocks = lax.axis_size("seq")
    split = w_out.shape[0] == HD and blocks == 4 * PLANE

    def partner(value, flip):
        return lax.ppermute(value, "seq", [(i, i ^ flip) for i in range(blocks)])

    def ring(value):
        return lax.ppermute(value, "seq", [(i, (i + PLANE) % blocks) for i in range(blocks)])

    def up(value, by):
        return lax.ppermute(value, "seq", [(i, i + by * PLANE) for i in range(blocks - by * PLANE)])

    def swap(value):
        return lax.ppermute(value, "mp", [(0, 1), (1, 0)])

    cols = w_out.shape[1]
    half = cols // 2

    def cut(block):
        return call(
            cut_kernel,
            [shape((HD, half), BF16), shape((HD, cols - half), BF16)],
            [ANY],
            [pltpu.SemaphoreType.DMA((2,))],
        )(block)

    held = {}
    if split:
        held["a0"], held["b0"] = cut(w_out)

    def piece(n):
        if n not in held:
            if n == "r1":
                held[n] = ring(w_out)
            elif n in ("a1", "b1"):
                held["a1"], held["b1"] = cut(piece("r1"))
            elif n[0] in "ab":
                held[n] = ring(piece(n[0] + str(int(n[1]) - 1)))
            else:
                held[n] = partner(piece({"x": "b", "y": "a"}[n[0]] + n[1]), {"x": 1, "y": 2}[n[0]])
        return held[n]

    def tied(value, name):
        names = DEADLINES.get(name, "").split() if split else []
        if not names:
            return value
        value, *rest = tie(value, *[piece(n) for n in names])
        held.update(zip(names, rest))
        return value

    per = heads // PLANE
    quarter = shape((per, HD, HD), BF16)
    own = call(states_kernel, [quarter] * PLANE, [VMEM, VMEM], flops=2 * rows * feats * HD)(keys, values)
    intra, feat = call(
        intra_kernel, [shape((rows, feats), F32), shape((rows, feats), BF16)], [VMEM] * 3, flops=4 * rows * rows * feats
    )(queries, keys, values)
    mine = [own[0]] + [partner(own[j], j) for j in range(1, PLANE)]
    mine[3] = tied(mine[3], "plane")
    (running,) = call(total_kernel, [quarter], [VMEM] * PLANE)(*mine)
    running = tied(running, "shift1")
    shifts, by = [], 1
    while by * PLANE < blocks:
        if by == 2:
            running = tied(running, "shift2")
        shifts.append(up(running, by))
        running = (running.astype(F32) + shifts[-1].astype(F32)).astype(BF16)
        by *= 2
    shifts[-1] = tied(shifts[-1], "shifted")
    prefixes = call(
        functools.partial(prefixes_kernel, len(shifts)), [quarter] * PLANE, [VMEM] * (PLANE + len(shifts))
    )(*mine, *shifts)
    prefixes = list(prefixes)
    prefixes[1] = tied(prefixes[1], "back")
    states = [prefixes[0]] + [partner(prefixes[j], j) for j in range(1, PLANE)]
    states[3] = tied(states[3], "states")
    gain = norm_gain.reshape(1, feats)
    normed_args = (intra, feat, *states, gain)

    if not split:
        (normed,) = call(norm_kernel, [shape((rows, feats), BF16)], [VMEM] * 7)(*normed_args)
        all_heads = lax.all_gather(normed, "mp", axis=1, tiled=True)
        weight = lax.all_gather(w_out, "seq", axis=0, tiled=True)
        return jnp.dot(all_heads, weight, preferred_element_type=F32).astype(BF16)

    normed, to_x, to_y = call(
        norm_send_kernel,
        [shape((rows, feats), BF16)] + [shape((rows, feats // 2), BF16)] * 2,
        [VMEM] * 7,
        flops=2 * rows * feats * HD,
    )(*normed_args)
    to_x = tied(to_x, "send")
    got_x, got_y = partner(to_x, 1), partner(to_y, 2)
    got_x = tied(got_x, "got_x")
    got_y = tied(got_y, "got_y")
    wa, wb = [], []
    for r in range(4):
        wa += [piece("a%d" % r), piece("y%d" % r)]
        wb += [piece("b%d" % r), piece("x%d" % r)]
    other = swap(normed)
    parts = []
    for flip, pieces, got in ((2, wa, got_x), (1, wb, got_y)):
        (part,) = call(
            functools.partial(partner_kernel, flip),
            [shape((rows, half), BF16)],
            [VMEM] * 10,
            [pltpu.VMEM((2, rows, feats // 2), BF16)],
            flops=rows * feats * half * 2,
        )(*pieces, got, swap(got))
        parts.append(partner(part, 3 - flip))
    (mine_all,) = call(
        own_kernel,
        [shape((rows, cols), F32)],
        [VMEM] * 18,
        [pltpu.VMEM((2, rows, feats), BF16)],
        flops=rows * feats * cols * 2,
    )(*wa, *wb, normed, other)
    result = None
    for at, part in ((half, parts[1]), (0, parts[0])):
        result = finish(mine_all, part, at, result)
    return result


def solution(mesh):
    in_specs = (P("seq", "mp"), P("seq", "mp"), P("seq", "mp"), P("mp"), P("seq", "mp"))
    out_specs = P("seq", "mp")
    return jax.shard_map(
        per_device, mesh=mesh, in_specs=in_specs, out_specs=out_specs, check_vma=False
    )
```

```python
import functools

import jax
import jax.numpy as jnp
from jax import lax
from jax.experimental import pallas as pl
from jax.experimental.pallas import tpu as pltpu
from jax.sharding import PartitionSpec as P

HD = 128
PLANE = 4
F32, BF16 = jnp.float32, jnp.bfloat16
VMEM_LIMIT = 40 * 1024 * 1024

ANY = pl.BlockSpec(memory_space=pl.ANY)
VMEM = pl.BlockSpec(memory_space=pltpu.VMEM)


def call(body, outs, ins, scratch=(), flops=0):
    return pl.pallas_call(
        body,
        out_shape=outs,
        in_specs=ins,
        out_specs=[VMEM] * len(outs),
        scratch_shapes=list(scratch),
        compiler_params=pltpu.CompilerParams(vmem_limit_bytes=VMEM_LIMIT),
        cost_estimate=pl.CostEstimate(flops=flops, bytes_accessed=0, transcendentals=0),
    )


def shape(dims, dtype):
    return jax.ShapeDtypeStruct(dims, dtype)


def spot():
    me = lax.axis_index("seq")
    return me % PLANE, me // PLANE, lax.axis_index("mp")


def silu(block):
    wide = block.astype(F32)
    return (wide / (1.0 + jnp.exp(-wide))).astype(BF16)


def head_cols(head):
    return pl.ds(pl.multiple_of(head * HD, HD), HD)


def states_kernel(k_ref, v_ref, *outs):
    place = spot()
    per = outs[0].shape[0]
    for j, out in enumerate(outs):
        quarter = place[0] ^ j
        for i in range(per):
            cols = head_cols(quarter * per + i)
            out[i] = lax.dot_general(
                silu(k_ref[:, cols]), v_ref[:, cols], (((0,), (0,)), ((), ())), preferred_element_type=F32
            ).astype(BF16)


def intra_kernel(q_ref, k_ref, v_ref, intra, feat):
    rows = q_ref.shape[0]
    causal = lax.broadcasted_iota(jnp.int32, (rows, rows), 0) >= lax.broadcasted_iota(jnp.int32, (rows, rows), 1)
    for h in range(q_ref.shape[1] // HD):
        cols = slice(h * HD, (h + 1) * HD)
        fq = silu(q_ref[:, cols])
        feat[:, cols] = fq
        scores = lax.dot_general(
            fq, silu(k_ref[:, cols]), (((1,), (1,)), ((), ())), preferred_element_type=F32
        )
        scores = jnp.where(causal, scores, 0.0).astype(BF16)
        intra[:, cols] = jnp.dot(scores, v_ref[:, cols], preferred_element_type=F32)


def total_kernel(a0, a1, a2, a3, out):
    out[...] = ((a0[...].astype(F32) + a1[...].astype(F32)) + (a2[...].astype(F32) + a3[...].astype(F32))).astype(BF16)


def prefixes_kernel(steps, *refs):
    place = spot()
    own, shifts, outs = refs[:PLANE], refs[PLANE:PLANE + steps], refs[PLANE + steps:]
    before = sum(ref[...].astype(F32) for ref in shifts)
    for j, out in enumerate(outs):
        total = before
        for i, ref in enumerate(own):
            total = total + jnp.where((place[0] ^ i) < (place[0] ^ j), ref[...].astype(F32), 0.0)
        out[...] = total.astype(BF16)


def norm_kernel(intra, feat, c0, c1, c2, c3, gain, normed):
    place = spot()
    for j, state in enumerate((c0, c1, c2, c3)):
        per = state.shape[0]
        for i in range(per):
            cols = head_cols((place[0] ^ j) * per + i)
            mixed = intra[:, cols] + jnp.dot(feat[:, cols], state[i], preferred_element_type=F32)
            scale = lax.rsqrt(jnp.mean(mixed * mixed, axis=-1, keepdims=True) + 1e-06)
            normed[:, cols] = (mixed * scale * gain[:, cols]).astype(BF16)


def norm_send_kernel(intra, feat, c0, c1, c2, c3, gain, normed, to_x, to_y):
    place = spot()
    norm_kernel(intra, feat, c0, c1, c2, c3, gain, normed)
    x, y = place[0] & 1, place[0] >> 1
    for t in range(4):
        slot = slice(t * HD, (t + 1) * HD)
        to_x[:, slot] = normed[:, head_cols(2 * t + (1 - x))]
        to_y[:, slot] = normed[:, head_cols(4 * (t // 2) + 2 * (1 - y) + t % 2)]


def head_at(place, r, t, flip):
    from_z = (place[1] - r) & 3
    return from_z >> 1, 4 * (from_z & 1) + (place[0] ^ (t * flip))


def sums(place, pieces, got, flip, thin):
    left = []
    for r in range(4):
        for t in range(2):
            core, head = head_at(place, r, t, flip)
            if thin:
                head = (head >> 1) if flip == 2 else 2 * (head >> 2) + (head & 1)
            cols = head_cols(head)
            left.append(got[core, :, cols])
    return jnp.dot(
        jnp.concatenate(left, axis=1), jnp.concatenate([p[...] for p in pieces], axis=0), preferred_element_type=F32
    )


def partner_kernel(flip, *refs):
    place = spot()
    own, other, out, got = refs[8:]
    got[place[2]] = own[...]
    got[1 - place[2]] = other[...]
    out[...] = sums(place, refs[:8], got, flip, True).astype(BF16)


def own_kernel(*refs):
    place = spot()
    own, other, out, got = refs[16:]
    got[place[2]] = own[...]
    got[1 - place[2]] = other[...]
    cut = refs[0].shape[1]
    out[:, :cut] = sums(place, refs[:8], got, 2, False)
    out[:, cut:] = sums(place, refs[8:16], got, 1, False)


def cut_kernel(block, first, second, sems):
    width = first.shape[1]
    copies = [
        pltpu.make_async_copy(block.at[:, pl.ds(0, width)], first, sems.at[0]),
        pltpu.make_async_copy(block.at[:, pl.ds(width, second.shape[1])], second, sems.at[1]),
    ]
    for copy in copies:
        copy.start()
    for copy in copies:
        copy.wait()


def finish_kernel(at, mine, part, *refs):
    out, held, sems = refs[-3:]
    rows, width = part.shape
    step = rows // 4
    copies = []
    for i in range(4):
        these = slice(i * step, (i + 1) * step)
        held[these] = (mine[these, at:at + width] + part[these].astype(F32)).astype(BF16)
        copies.append(
            pltpu.make_async_copy(
                held.at[pl.ds(i * step, step)], out.at[pl.ds(i * step, step), pl.ds(at, width)], sems.at[i]
            )
        )
        copies[-1].start()
    for copy in copies:
        copy.wait()


def finish(mine, part, at, result):
    return pl.pallas_call(
        functools.partial(finish_kernel, at),
        out_shape=shape(mine.shape, BF16),
        in_specs=[VMEM] * 2 + ([ANY] if result is not None else []),
        out_specs=ANY,
        scratch_shapes=[pltpu.VMEM(part.shape, BF16), pltpu.SemaphoreType.DMA((4,))],
        input_output_aliases={2: 0} if result is not None else {},
        compiler_params=pltpu.CompilerParams(vmem_limit_bytes=VMEM_LIMIT),
    )(*([mine, part] + ([result] if result is not None else [])))


DEADLINES = {'shift1': 'y0', 'shifted': 'a2 x0', 'back': 'x1', 'states': 'y1', 'got_x': 'a3 x2 y3', 'got_y': 'b3'}


def tie(value, *others):
    return lax.optimization_barrier((value, *others))


def per_device(queries, keys, values, norm_gain, w_out):
    rows, feats = queries.shape
    heads = feats // HD
    blocks = lax.axis_size("seq")
    split = w_out.shape[0] == HD and blocks == 4 * PLANE

    def partner(value, flip):
        return lax.ppermute(value, "seq", [(i, i ^ flip) for i in range(blocks)])

    def ring(value):
        return lax.ppermute(value, "seq", [(i, (i + PLANE) % blocks) for i in range(blocks)])

    def up(value, by):
        return lax.ppermute(value, "seq", [(i, i + by * PLANE) for i in range(blocks - by * PLANE)])

    def swap(value):
        return lax.ppermute(value, "mp", [(0, 1), (1, 0)])

    cols = w_out.shape[1]
    half = cols // 2

    def cut(block):
        return call(
            cut_kernel,
            [shape((HD, half), BF16), shape((HD, cols - half), BF16)],
            [ANY],
            [pltpu.SemaphoreType.DMA((2,))],
        )(block)

    held = {}
    if split:
        held["a0"], held["b0"] = cut(w_out)

    def piece(n):
        if n not in held:
            if n == "r1":
                held[n] = ring(w_out)
            elif n in ("a1", "b1"):
                held["a1"], held["b1"] = cut(piece("r1"))
            elif n[0] in "ab":
                held[n] = ring(piece(n[0] + str(int(n[1]) - 1)))
            else:
                held[n] = partner(piece({"x": "b", "y": "a"}[n[0]] + n[1]), {"x": 1, "y": 2}[n[0]])
        return held[n]

    def tied(value, name):
        names = DEADLINES.get(name, "").split() if split else []
        if not names:
            return value
        value, *rest = tie(value, *[piece(n) for n in names])
        held.update(zip(names, rest))
        return value

    per = heads // PLANE
    quarter = shape((per, HD, HD), BF16)
    own = call(states_kernel, [quarter] * PLANE, [VMEM, VMEM], flops=2 * rows * feats * HD)(keys, values)
    intra, feat = call(
        intra_kernel, [shape((rows, feats), F32), shape((rows, feats), BF16)], [VMEM] * 3, flops=4 * rows * rows * feats
    )(queries, keys, values)
    mine = [own[0]] + [partner(own[j], j) for j in range(1, PLANE)]
    mine[3] = tied(mine[3], "plane")
    (running,) = call(total_kernel, [quarter], [VMEM] * PLANE)(*mine)
    running = tied(running, "shift1")
    shifts, by = [], 1
    while by * PLANE < blocks:
        if by == 2:
            running = tied(running, "shift2")
        shifts.append(up(running, by))
        running = (running.astype(F32) + shifts[-1].astype(F32)).astype(BF16)
        by *= 2
    shifts[-1] = tied(shifts[-1], "shifted")
    prefixes = call(
        functools.partial(prefixes_kernel, len(shifts)), [quarter] * PLANE, [VMEM] * (PLANE + len(shifts))
    )(*mine, *shifts)
    prefixes = list(prefixes)
    prefixes[1] = tied(prefixes[1], "back")
    states = [prefixes[0]] + [partner(prefixes[j], j) for j in range(1, PLANE)]
    states[3] = tied(states[3], "states")
    gain = norm_gain.reshape(1, feats)
    normed_args = (intra, feat, *states, gain)

    if not split:
        (normed,) = call(norm_kernel, [shape((rows, feats), BF16)], [VMEM] * 7)(*normed_args)
        all_heads = lax.all_gather(normed, "mp", axis=1, tiled=True)
        weight = lax.all_gather(w_out, "seq", axis=0, tiled=True)
        return jnp.dot(all_heads, weight, preferred_element_type=F32).astype(BF16)

    normed, to_x, to_y = call(
        norm_send_kernel,
        [shape((rows, feats), BF16)] + [shape((rows, feats // 2), BF16)] * 2,
        [VMEM] * 7,
        flops=2 * rows * feats * HD,
    )(*normed_args)
    to_x = tied(to_x, "send")
    other = swap(normed)
    got_y, got_x = partner(to_y, 2), partner(to_x, 1)
    got_x = tied(got_x, "got_x")
    got_y = tied(got_y, "got_y")
    wa, wb = [], []
    for r in range(4):
        wa += [piece("a%d" % r), piece("y%d" % r)]
        wb += [piece("b%d" % r), piece("x%d" % r)]
    parts = []
    for flip, pieces, got in ((2, wa, got_x), (1, wb, got_y)):
        (part,) = call(
            functools.partial(partner_kernel, flip),
            [shape((rows, half), BF16)],
            [VMEM] * 10,
            [pltpu.VMEM((2, rows, feats // 2), BF16)],
            flops=rows * feats * half * 2,
        )(*pieces, got, swap(got))
        parts.append(partner(part, 3 - flip))
    (mine_all,) = call(
        own_kernel,
        [shape((rows, cols), F32)],
        [VMEM] * 18,
        [pltpu.VMEM((2, rows, feats), BF16)],
        flops=rows * feats * cols * 2,
    )(*wa, *wb, normed, other)
    result = None
    for at, part in ((half, parts[1]), (0, parts[0])):
        result = finish(mine_all, part, at, result)
    return result


def solution(mesh):
    in_specs = (P("seq", "mp"), P("seq", "mp"), P("seq", "mp"), P("mp"), P("seq", "mp"))
    out_specs = P("seq", "mp")
    return jax.shard_map(
        per_device, mesh=mesh, in_specs=in_specs, out_specs=out_specs, check_vma=False
    )
```
